512 devices in a mesh: shot: 16 (over x, z_hi), head: 32 (over z_lo, y, core).
Axes of the slice: x: 4, y: 4, z: 16 (z_hi: 4, z_lo: 4; z = z_hi * 4 + z_lo), core: 2. Of those that a mesh axis runs over, the one named last changes fastest.
Arguments:
- queries: bfloat16 [16, 2048, 4096], P('shot', 'head'), may hold values from -22 to 22
- key_rows: bfloat16 [16, 2048, 4096], P('shot', 'head'), may hold values from -4 to 4
- value_rows: bfloat16 [16, 2048, 4096], P('shot', 'head'), may hold values from -5 to 5
- shot_lengths: int32 [16], replicated, may hold values from 1024 to 2048, as said below
- shot_links: int32 [2, 16], replicated, may hold values 0 or 1
- block_select: int32 [2, 16, 2], replicated, may hold values from 0 to 15, as said below
Outputs:
- attended: bfloat16 [16, 2048, 4096], P('shot', 'head')
The draws below stay inside these ranges and needn't reach their ends.
Inputs may be any that keep to these rules, and one draw needn't show every extreme that they name: `shot_lengths`: multiples of 128; some shot has exactly 2048 tokens and some exactly 1024. `block_select`: the 2 blocks of one [r, s] are different and lie wholly below the length of shot s XOR (16 >> (r + 1)).
All inputs are finite; a program needn't handle non-finite values.
Results may differ from the reference program's by a relative error of at most 0.0047.
Values may be sent and summed in bfloat16 or wider, within the bound.
No kernel may reach another device: no remote copies, remote signals or barrier semaphores. Data moves between devices by JAX's collectives and lax.ppermute only.
A program may use at most 64 MiB of HBM per device.

```python
import jax
import jax.numpy as jnp
from jax import lax

HEADS = 32
HEAD_DIM = 128
LMAX = 2048
BLK = 128
SEL = 2
ROUNDS = 2
SHOTS = 16


def shared_counts(key):
    key = jax.random.fold_in(key, 5)
    blocks = LMAX // BLK
    counts = jax.random.randint(key, (SHOTS,), blocks // 2, blocks + 1)
    order = jax.random.permutation(jax.random.fold_in(key, 6), SHOTS)
    counts = counts.at[order[0]].set(blocks).at[order[1]].set(blocks // 2)
    return (counts, order)


def draw_queries(key, part):
    key = jax.random.fold_in(key, 11)
    shape = (SHOTS, LMAX, HEADS * HEAD_DIM)
    return jnp.clip(jax.random.normal(key, shape, jnp.float32), -4.0, 4.0).astype(jnp.bfloat16)


def draw_key_rows(key, part):
    key = jax.random.fold_in(key, 13)
    shape = (SHOTS, LMAX, HEADS * HEAD_DIM)
    return jnp.clip(jax.random.normal(key, shape, jnp.float32), -4.0, 4.0).astype(jnp.bfloat16)


def draw_shot_lengths(key, part):
    counts, order = shared_counts(key)
    return (counts * BLK).astype(jnp.int32)


def draw_block_select(key, part):
    counts, order = shared_counts(key)
    key = jax.random.fold_in(key, 31)
    blocks = LMAX // BLK
    shots = jnp.arange(SHOTS, dtype=jnp.int32)
    strides = jnp.array([SHOTS >> r + 1 for r in range(ROUNDS)], dtype=jnp.int32)
    partners = jnp.bitwise_xor(shots[None, :], strides[:, None])
    valid_blocks = counts[partners]
    raw = jax.random.randint(key, (ROUNDS, SHOTS, blocks), 0, 1 << 20)
    index = jnp.arange(blocks, dtype=jnp.int32)
    scores = raw * blocks + index[None, None, :] + jnp.where(index[None, None, :] < valid_blocks[:, :, None], 0, 1 << 30)
    full_taker = jnp.bitwise_xor(order[0], jnp.int32(SHOTS >> 1))
    half_taker = jnp.bitwise_xor(order[1], jnp.int32(SHOTS >> 1))
    scores = scores.at[0, full_taker, blocks - 1].set(-1)
    scores = scores.at[0, half_taker, 0].set(-1)
    ranked = jnp.argsort(scores, axis=2, stable=True)
    return ranked[:, :, :SEL].astype(jnp.int32)


def with_ends(values, key, smallest, largest):
    spot = [jax.random.randint(jax.random.fold_in(key, axis), (), 0, length) for axis, length in enumerate(values.shape)]
    longest = values.shape.index(max(values.shape))
    next_to = spot[:longest] + [(spot[longest] + 1) % values.shape[longest]] + spot[longest + 1:]
    return values.at[tuple(spot)].set(smallest).at[tuple(next_to)].set(largest)


def block_levels(rng, dims, pieces, low, high):
    loudness, own = 1.0, jax.random.fold_in(rng, 6)
    for dim, blocks in pieces:
        draws = jnp.exp(jax.random.uniform(jax.random.fold_in(own, dim), (blocks,), jnp.float32, low / len(pieces), high / len(pieces)))
        loudness = loudness * jnp.repeat(draws, dims[dim] // blocks).reshape([-1 if axis == dim else 1 for axis in range(len(dims))])
    return loudness


def gaussian(own_key, shape, scale, most, shards=(), held_as=jnp.bfloat16):
    drawn = jax.random.normal(own_key, shape, jnp.float32) * scale
    if len(shards) > 0:
        drawn = block_levels(own_key, shape, shards, -0.22, 0.18) * drawn
    return jnp.clip(drawn, min=-most, max=most).astype(held_as)


def setup_inputs(seed: int = 0) -> dict:
    key_of = jax.random.split(jax.random.key(seed), 7)
    return {
        "queries": draw_queries(jax.random.fold_in(key_of[6], 71), 0),
        "key_rows": draw_key_rows(jax.random.fold_in(key_of[6], 71), 0),
        "value_rows": gaussian(key_of[2], (SHOTS, LMAX, HEADS * HEAD_DIM), 1.0, 5.0, ((0, 16), (1, 32))),
        "shot_lengths": draw_shot_lengths(jax.random.fold_in(key_of[6], 71), 0),
        "shot_links": with_ends((jax.random.randint(key_of[4], (ROUNDS, SHOTS), 0, 2) < 1).astype(jnp.int32), jax.random.fold_in(key_of[4], 1), 0, 1),
        "block_select": draw_block_select(jax.random.fold_in(key_of[6], 71), 0),
    }


def take_blocks(source, chosen):
    feature_width = source.shape[1]
    shaped = source.reshape(source.shape[0] // BLK, BLK, feature_width)
    return shaped[chosen].reshape(chosen.shape[0] * BLK, feature_width)


def attend(query_rows, key_all, value_all, key_bias):
    length = query_rows.shape[0]
    feature_width = query_rows.shape[1]
    head_count = feature_width // HEAD_DIM
    query_heads = query_rows.reshape(length, head_count, HEAD_DIM).astype(jnp.float32)
    key_heads = key_all.reshape(-1, head_count, HEAD_DIM).astype(jnp.float32)
    value_heads = value_all.reshape(-1, head_count, HEAD_DIM).astype(jnp.float32)
    block_rows = min(512, length)
    scale = HEAD_DIM ** -0.5

    def block_attend(query_block):
        scores = jnp.einsum("qhd,khd->hqk", query_block, key_heads, precision=lax.Precision.HIGHEST) * scale + key_bias
        row_max = jnp.max(scores, axis=2, keepdims=True)
        exp_terms = jnp.exp(scores - row_max)
        denominator = jnp.sum(exp_terms, axis=2)
        weights = lax.optimization_barrier(exp_terms.astype(jnp.bfloat16)).astype(jnp.float32)
        weighted = jnp.einsum("hqk,khd->qhd", weights, value_heads, precision=lax.Precision.HIGHEST)
        return weighted / jnp.transpose(denominator)[:, :, None]

    blocks = query_heads.reshape(length // block_rows, block_rows, head_count, HEAD_DIM)
    return lax.map(block_attend, blocks).reshape(length, feature_width)


def reference(queries, key_rows, value_rows, shot_lengths, shot_links, block_select):
    positions = jnp.arange(LMAX, dtype=jnp.int32)
    far_count = SEL * BLK

    def per_shot(shot_index):
        own_length = shot_lengths[shot_index]
        key_parts = [key_rows[shot_index]]
        value_parts = [value_rows[shot_index]]
        bias_parts = [jnp.where(positions < own_length, jnp.zeros((LMAX,), jnp.float32), jnp.full((LMAX,), -1e30, jnp.float32))]
        for round_index in range(ROUNDS):
            partner = jnp.bitwise_xor(shot_index, jnp.int32(SHOTS >> (round_index + 1)))
            chosen = block_select[round_index, shot_index]
            key_parts.append(take_blocks(key_rows[partner], chosen))
            value_parts.append(take_blocks(value_rows[partner], chosen))
            linked = shot_links[round_index, shot_index]
            bias_parts.append(jnp.where(linked > 0, jnp.zeros((far_count,), jnp.float32), jnp.full((far_count,), -1e30, jnp.float32)))
        result = attend(queries[shot_index], jnp.concatenate(key_parts, axis=0), jnp.concatenate(value_parts, axis=0), jnp.concatenate(bias_parts, axis=0))
        live = (positions < own_length)[:, None]
        return jnp.where(live, result, jnp.zeros_like(result)).astype(jnp.bfloat16)

    return lax.map(per_shot, jnp.arange(SHOTS, dtype=jnp.int32))
```

```python
import jax
import jax.numpy as jnp
from jax import lax
from jax.experimental import pallas as pl
from jax.experimental.pallas import tpu as pltpu
from jax.sharding import PartitionSpec as P

HEAD_DIM = 128
LMAX = 2048
LMIN = 1024
BLK = 128
SEL = 2
ROUNDS = 2
SHOTS = 16
FAR = SEL * BLK
SCALE = HEAD_DIM ** (-0.5)
LOG2E = 1.4426950408889634
NEG = -1e30
CHUNK = 256
SUB = 256
VMEM_BYTES = 24 << 20
SMALL_BYTES = 6 << 20


def split_heads_kernel(*refs):
    *sources, out_ref = refs
    heads, _, _ = out_ref.shape
    rows = sources[0].shape[0]
    for number, source in enumerate(sources):
        for head in range(heads):
            out_ref[head, number * rows : (number + 1) * rows, :] = source[
                :, head * HEAD_DIM : (head + 1) * HEAD_DIM
            ]


def split_heads(*arrays):
    rows, width = arrays[0].shape
    heads = width // HEAD_DIM
    return pl.pallas_call(
        split_heads_kernel,
        in_specs=[pl.BlockSpec(memory_space=pltpu.VMEM)] * len(arrays),
        out_specs=pl.BlockSpec(memory_space=pltpu.VMEM),
        out_shape=jax.ShapeDtypeStruct((heads, len(arrays) * rows, HEAD_DIM), jnp.bfloat16),
        compiler_params=pltpu.CompilerParams(vmem_limit_bytes=SMALL_BYTES),
        name="split_heads",
    )(*arrays)


def join_heads_kernel(source, out_ref):
    heads, _, _ = source.shape
    for head in range(heads):
        out_ref[:, head * HEAD_DIM : (head + 1) * HEAD_DIM] = source[head]


def join_heads(array):
    heads, rows, _ = array.shape
    return pl.pallas_call(
        join_heads_kernel,
        in_specs=[pl.BlockSpec(memory_space=pltpu.VMEM)],
        out_specs=pl.BlockSpec(memory_space=pltpu.VMEM),
        out_shape=jax.ShapeDtypeStruct((rows, heads * HEAD_DIM), jnp.bfloat16),
        compiler_params=pltpu.CompilerParams(vmem_limit_bytes=SMALL_BYTES),
        name="join_heads",
    )(array)


def pick_kernel(block_select, own_ref, *outs):
    shot = lax.axis_index("shot")
    piece = own_ref.shape[1] // 2
    group = BLK // piece
    for round_index, out_ref in enumerate(outs):
        partner = shot ^ (SHOTS >> (round_index + 1))
        for pick in range(SEL):
            first = block_select[round_index, partner, pick] * group
            out_ref[pick * group : (pick + 1) * group] = own_ref[pl.ds(first, group)]


def pick_blocks(block_select, own):
    shape = jax.ShapeDtypeStruct((FAR // (own.shape[1] // 2),) + own.shape[1:], jnp.bfloat16)
    return pl.pallas_call(
        pick_kernel,
        in_specs=[
            pl.BlockSpec(memory_space=pltpu.SMEM),
            pl.BlockSpec(memory_space=pltpu.VMEM),
        ],
        out_specs=[pl.BlockSpec(memory_space=pltpu.VMEM)] * ROUNDS,
        out_shape=[shape] * ROUNDS,
        compiler_params=pltpu.CompilerParams(vmem_limit_bytes=SMALL_BYTES),
        name="pick_blocks",
    )(block_select, own)


def attend_kernel(lengths, links, query_ref, own_ref, *refs):
    *far_refs, out_ref, value_ref = refs
    shot = lax.axis_index("shot")
    length = lengths[shot]
    piece = query_ref.shape[1]
    group = CHUNK // piece
    lane = lax.broadcasted_iota(jnp.int32, (1, CHUNK), 1)
    keys, bias = [], []

    def add_keys(source, first, shift):
        place = slice(first, first + group)
        spot = slice(len(keys) * CHUNK, (len(keys) + 1) * CHUNK)
        keys.append(source[place, 0:piece, :].reshape(CHUNK, HEAD_DIM))
        value_ref[spot, :HEAD_DIM] = source[place, piece : 2 * piece, :].reshape(CHUNK, HEAD_DIM)
        value_ref[spot, HEAD_DIM:] = jnp.ones((CHUNK, HEAD_DIM), jnp.bfloat16)
        bias.append(shift)

    for chunk in range(LMAX // CHUNK):
        shift = None
        if (chunk + 1) * CHUNK > LMIN:
            shift = jnp.where(lane + chunk * CHUNK < length, 0.0, NEG).astype(jnp.float32)
        add_keys(own_ref, chunk * group, shift)
    for round_index, far_ref in enumerate(far_refs):
        shift = jnp.where(links[round_index, shot] > 0, 0.0, NEG).astype(jnp.float32)
        for chunk in range(FAR // CHUNK):
            add_keys(far_ref, chunk * group, shift)

    parts = LMAX // SUB
    scores, row_max = None, None
    for part in range(parts + 1):
        new_scores, top, weighted = [], None, None
        if part < parts:
            place = slice(part * SUB // piece, (part + 1) * SUB // piece)
            query = query_ref[place].reshape(SUB, HEAD_DIM)
        for chunk, (key, shift) in enumerate(zip(keys, bias)):
            if part < parts:
                score = lax.dot_general(
                    query, key, (((1,), (1,)), ((), ())), preferred_element_type=jnp.float32
                )
                if shift is not None:
                    score = score + shift
                new_scores.append(score)
                top = score if top is None else jnp.maximum(top, score)
            if part > 0:
                terms = jnp.exp2(scores[chunk] * (SCALE * LOG2E) - row_max)
                product = jnp.dot(
                    terms.astype(jnp.bfloat16),
                    value_ref[chunk * CHUNK : (chunk + 1) * CHUNK, :],
                    preferred_element_type=jnp.float32,
                )
                weighted = product if weighted is None else weighted + product
        if part > 0:
            first = (part - 1) * SUB
            position = first + lax.broadcasted_iota(jnp.int32, (SUB, 1), 0)
            result = weighted[:, :HEAD_DIM] / weighted[:, HEAD_DIM : HEAD_DIM + 1]
            result = jnp.where(position < length, result, 0.0).astype(jnp.bfloat16)
            out_ref[first // piece : (first + SUB) // piece] = result.reshape(
                SUB // piece, piece, HEAD_DIM
            )
        if part < parts:
            scores, row_max = new_scores, jnp.max(top, axis=1, keepdims=True) * (SCALE * LOG2E)


def attend(lengths, links, query, own, *far):
    keys = LMAX + ROUNDS * FAR
    smem = pl.BlockSpec(memory_space=pltpu.SMEM)
    vmem = pl.BlockSpec(memory_space=pltpu.VMEM)
    return pl.pallas_call(
        attend_kernel,
        in_specs=[smem, smem] + [vmem] * (2 + ROUNDS),
        out_specs=vmem,
        out_shape=jax.ShapeDtypeStruct(query.shape, jnp.bfloat16),
        scratch_shapes=[pltpu.VMEM((keys, 2 * HEAD_DIM), jnp.bfloat16)],
        compiler_params=pltpu.CompilerParams(vmem_limit_bytes=VMEM_BYTES),
        cost_estimate=pl.CostEstimate(
            flops=4 * LMAX * keys * HEAD_DIM, bytes_accessed=2 << 20, transcendentals=LMAX * keys
        ),
        name="attend",
    )(lengths, links, query, own, *far)


def swap(array):
    return lax.all_to_all(array, "head", split_axis=0, concat_axis=0, tiled=True)


def from_partner(array, bit):
    count = lax.axis_size("shot")
    return lax.ppermute(array, "shot", [(low, low ^ bit) for low in range(count)])


def body(queries, key_rows, value_rows, shot_lengths, shot_links, block_select):
    own = swap(split_heads(key_rows[0], value_rows[0]))
    query = swap(split_heads(queries[0]))
    far = [
        from_partner(picked, SHOTS >> (round_index + 1))
        for round_index, picked in enumerate(pick_blocks(block_select, own))
    ]
    result = attend(shot_lengths, shot_links, query, own, *far)
    return join_heads(swap(result))[None]


def solution(mesh):
    placed = (
        P("shot", "head", None),
        P("shot", "head", None),
        P("shot", "head", None),
        P(),
        P(),
        P(),
    )
    return jax.shard_map(
        body, mesh=mesh, in_specs=placed, out_specs=P("shot", "head", None), check_vma=False
    )
```

```python
import jax
import jax.numpy as jnp
from jax import lax
from jax.experimental import pallas as pl
from jax.experimental.pallas import tpu as pltpu
from jax.sharding import PartitionSpec as P

HEAD_DIM = 128
LMAX = 2048
LMIN = 1024
BLK = 128
SEL = 2
ROUNDS = 2
SHOTS = 16
FAR = SEL * BLK
FACTOR = HEAD_DIM ** (-0.5) * 1.4426950408889634
CHUNK = 256
SUB = 256
HEADS_A_STEP = 4
VMEM_BYTES = 24 << 20
SMALL_BYTES = 6 << 20
LARGE_BYTES = 60 << 20


def split_heads_kernel(*refs):
    count = len(refs) - 5
    sources, out_ref, held, made, come, gone = refs[:count], *refs[count:]
    rows = held.shape[1]
    wide = HEADS_A_STEP * HEAD_DIM
    steps = out_ref.shape[0] // HEADS_A_STEP
    arrivals = [
        [
            pltpu.make_async_copy(
                source.at[:, pl.ds(step * wide, wide)],
                held.at[number, :, pl.ds(step * wide, wide)],
                come.at[number, step],
            )
            for number, source in enumerate(sources)
        ]
        for step in range(steps)
    ]
    for step in arrivals:
        for arrival in step:
            arrival.start()
    leaving = []
    for step in range(steps):
        place = pl.ds(step * HEADS_A_STEP, HEADS_A_STEP)
        for number in range(count):
            arrivals[step][number].wait()
            for head in range(step * HEADS_A_STEP, (step + 1) * HEADS_A_STEP):
                made[head, number * rows : (number + 1) * rows, :] = held[
                    number, :, head * HEAD_DIM : (head + 1) * HEAD_DIM
                ]
        copy = pltpu.make_async_copy(made.at[place], out_ref.at[place], gone.at[step])
        copy.start()
        leaving.append(copy)
    for copy in leaving:
        copy.wait()


def split_heads(*arrays, vmem_bytes=SMALL_BYTES):
    count = len(arrays)
    rows, width = arrays[0].shape
    heads = width // HEAD_DIM
    steps = heads // HEADS_A_STEP
    shape = (heads, count * rows, HEAD_DIM)
    return pl.pallas_call(
        split_heads_kernel,
        in_specs=[pl.BlockSpec(memory_space=pltpu.HBM)] * count,
        out_specs=pl.BlockSpec(memory_space=pltpu.HBM),
        out_shape=jax.ShapeDtypeStruct(shape, jnp.bfloat16),
        scratch_shapes=[
            pltpu.VMEM((count, rows, width), jnp.bfloat16),
            pltpu.VMEM(shape, jnp.bfloat16),
            pltpu.SemaphoreType.DMA((count, steps)),
            pltpu.SemaphoreType.DMA((steps,)),
        ],
        compiler_params=pltpu.CompilerParams(vmem_limit_bytes=vmem_bytes),
        name="split_heads",
    )(*arrays)


def join_heads_kernel(source, out_ref):
    heads, _, _ = source.shape
    for head in range(heads):
        out_ref[:, head * HEAD_DIM : (head + 1) * HEAD_DIM] = source[head]


def join_heads(array):
    heads, rows, _ = array.shape
    return pl.pallas_call(
        join_heads_kernel,
        in_specs=[pl.BlockSpec(memory_space=pltpu.VMEM)],
        out_specs=pl.BlockSpec(memory_space=pltpu.VMEM),
        out_shape=jax.ShapeDtypeStruct((rows, heads * HEAD_DIM), jnp.bfloat16),
        compiler_params=pltpu.CompilerParams(vmem_limit_bytes=SMALL_BYTES),
        name="join_heads",
    )(array)


def pick_kernel(block_select, own_ref, *outs):
    shot = lax.axis_index("shot")
    piece = own_ref.shape[1] // 2
    group = BLK // piece
    for round_index, out_ref in enumerate(outs):
        partner = shot ^ (SHOTS >> (round_index + 1))
        for pick in range(SEL):
            first = block_select[round_index, partner, pick] * group
            out_ref[pick * group : (pick + 1) * group] = own_ref[pl.ds(first, group)]


def pick_blocks(block_select, own):
    shape = jax.ShapeDtypeStruct((FAR // (own.shape[1] // 2),) + own.shape[1:], jnp.bfloat16)
    return pl.pallas_call(
        pick_kernel,
        in_specs=[
            pl.BlockSpec(memory_space=pltpu.SMEM),
            pl.BlockSpec(memory_space=pltpu.VMEM),
        ],
        out_specs=[pl.BlockSpec(memory_space=pltpu.VMEM)] * ROUNDS,
        out_shape=[shape] * ROUNDS,
        compiler_params=pltpu.CompilerParams(vmem_limit_bytes=SMALL_BYTES),
        name="pick_blocks",
    )(block_select, own)


def attend_kernel(lengths, links, query_ref, own_ref, *refs):
    *far_refs, out_ref = refs
    shot = lax.axis_index("shot")
    length = lengths[shot]
    piece = query_ref.shape[1]
    group = BLK // piece
    blocks = []
    for block in range(LMAX // BLK):
        live = None if (block + 1) * BLK <= LMIN else block * BLK < length
        blocks.append((own_ref, block * group, live))
    for round_index, far_ref in enumerate(far_refs):
        for pick in range(SEL):
            blocks.append((far_ref, pick * group, links[round_index, shot] > 0))
    chunks = [blocks[n : n + CHUNK // BLK] for n in range(0, len(blocks), CHUNK // BLK)]

    def keys_of(chunk):
        parts = []
        for source, first, live in chunk:
            part = source[first : first + group, 0:piece, :].reshape(BLK, HEAD_DIM)
            if live is not None:
                part = jnp.where(live, part, own_ref[0:group, 0:piece, :].reshape(BLK, HEAD_DIM))
            parts.append(part)
        key = jnp.concatenate(parts, axis=0)
        return jnp.concatenate([key, key], axis=1)

    def values_of(chunk):
        parts = []
        for source, first, live in chunk:
            part = source[first : first + group, piece : 2 * piece, :].reshape(BLK, HEAD_DIM)
            part = jnp.concatenate([part, jnp.ones_like(part)], axis=1)
            parts.append(part if live is None else jnp.where(live, part, jnp.zeros_like(part)))
        return jnp.concatenate(parts, axis=0)

    parts = LMAX // SUB
    scores, row_max = None, None
    for part in range(parts + 1):
        new_scores, top, weighted = [], None, None
        if part < parts:
            place = slice(part * SUB // piece, (part + 1) * SUB // piece)
            scaled = query_ref[place].reshape(SUB, HEAD_DIM).astype(jnp.float32) * FACTOR
            high = scaled.astype(jnp.bfloat16)
            low = (scaled - high.astype(jnp.float32)).astype(jnp.bfloat16)
            query = jnp.concatenate([high, low], axis=1)
        for number, chunk in enumerate(chunks):
            if part < parts:
                score = lax.dot_general(
                    query,
                    keys_of(chunk),
                    (((1,), (1,)), ((), ())),
                    preferred_element_type=jnp.float32,
                )
                new_scores.append(score)
                top = score if top is None else jnp.maximum(top, score)
            if part > 0:
                terms = jnp.exp2(scores[number] - row_max).astype(jnp.bfloat16)
                product = jnp.dot(terms, values_of(chunk), preferred_element_type=jnp.float32)
                weighted = product if weighted is None else weighted + product
        if part > 0:
            first = (part - 1) * SUB
            position = first + lax.broadcasted_iota(jnp.int32, (SUB, 1), 0)
            result = weighted[:, :HEAD_DIM] / weighted[:, HEAD_DIM : HEAD_DIM + 1]
            result = jnp.where(position < length, result, 0.0).astype(jnp.bfloat16)
            out_ref[first // piece : (first + SUB) // piece] = result.reshape(
                SUB // piece, piece, HEAD_DIM
            )
        if part < parts:
            scores, row_max = new_scores, jnp.max(top, axis=1, keepdims=True)


def attend(lengths, links, query, own, *far):
    keys = LMAX + ROUNDS * FAR
    smem = pl.BlockSpec(memory_space=pltpu.SMEM)
    vmem = pl.BlockSpec(memory_space=pltpu.VMEM)
    return pl.pallas_call(
        attend_kernel,
        in_specs=[smem, smem] + [vmem] * (2 + ROUNDS),
        out_specs=vmem,
        out_shape=jax.ShapeDtypeStruct(query.shape, jnp.bfloat16),
        compiler_params=pltpu.CompilerParams(vmem_limit_bytes=VMEM_BYTES),
        cost_estimate=pl.CostEstimate(
            flops=4 * LMAX * keys * HEAD_DIM, bytes_accessed=2 << 20, transcendentals=LMAX * keys
        ),
        name="attend",
    )(lengths, links, query, own, *far)


def swap(array):
    return lax.all_to_all(array, "head", split_axis=0, concat_axis=0, tiled=True)


def from_partner(array, bit):
    count = lax.axis_size("shot")
    return lax.ppermute(array, "shot", [(low, low ^ bit) for low in range(count)])


def body(queries, key_rows, value_rows, shot_lengths, shot_links, block_select):
    own = swap(split_heads(key_rows[0], value_rows[0], vmem_bytes=LARGE_BYTES))
    query = swap(split_heads(queries[0]))
    far = [
        from_partner(picked, SHOTS >> (round_index + 1))
        for round_index, picked in enumerate(pick_blocks(block_select, own))
    ]
    result = attend(shot_lengths, shot_links, query, own, *far)
    return join_heads(swap(result))[None]


def solution(mesh):
    placed = (
        P("shot", "head", None),
        P("shot", "head", None),
        P("shot", "head", None),
        P(),
        P(),
        P(),
    )
    return jax.shard_map(
        body, mesh=mesh, in_specs=placed, out_specs=P("shot", "head", None), check_vma=False
    )
```

```python
import functools

import jax
import jax.numpy as jnp
from jax import lax
from jax.experimental import pallas as pl
from jax.experimental.pallas import tpu as pltpu
from jax.sharding import PartitionSpec as P

HEAD_DIM = 128
LMAX = 2048
LMIN = 1024
BLK = 128
SEL = 2
ROUNDS = 2
SHOTS = 16
FAR = SEL * BLK
FACTOR = HEAD_DIM ** (-0.5) * 1.4426950408889634
CHUNK = 256
SUB = 256
HEADS_A_STEP = 4
VMEM_BYTES = 24 << 20
SMALL_BYTES = 6 << 20
LARGE_BYTES = 60 << 20


def split_heads_kernel(*refs):
    count = len(refs) - 5
    sources, out_ref, held, made, come, gone = refs[:count], *refs[count:]
    rows = held.shape[1]
    wide = HEADS_A_STEP * HEAD_DIM
    steps = out_ref.shape[0] // HEADS_A_STEP
    arrivals = [
        [
            pltpu.make_async_copy(
                source.at[:, pl.ds(step * wide, wide)],
                held.at[number, :, pl.ds(step * wide, wide)],
                come.at[number, step],
            )
            for number, source in enumerate(sources)
        ]
        for step in range(steps)
    ]
    for step in arrivals:
        for arrival in step:
            arrival.start()
    leaving = []
    for step in range(steps):
        place = pl.ds(step * HEADS_A_STEP, HEADS_A_STEP)
        for number in range(count):
            arrivals[step][number].wait()
            for head in range(step * HEADS_A_STEP, (step + 1) * HEADS_A_STEP):
                made[head, number * rows : (number + 1) * rows, :] = held[
                    number, :, head * HEAD_DIM : (head + 1) * HEAD_DIM
                ]
        copy = pltpu.make_async_copy(made.at[place], out_ref.at[place], gone.at[step])
        copy.start()
        leaving.append(copy)
    for copy in leaving:
        copy.wait()


def split_heads(*arrays, vmem_bytes=SMALL_BYTES):
    count = len(arrays)
    rows, width = arrays[0].shape
    heads = width // HEAD_DIM
    steps = heads // HEADS_A_STEP
    shape = (heads, count * rows, HEAD_DIM)
    return pl.pallas_call(
        split_heads_kernel,
        in_specs=[pl.BlockSpec(memory_space=pltpu.HBM)] * count,
        out_specs=pl.BlockSpec(memory_space=pltpu.HBM),
        out_shape=jax.ShapeDtypeStruct(shape, jnp.bfloat16),
        scratch_shapes=[
            pltpu.VMEM((count, rows, width), jnp.bfloat16),
            pltpu.VMEM(shape, jnp.bfloat16),
            pltpu.SemaphoreType.DMA((count, steps)),
            pltpu.SemaphoreType.DMA((steps,)),
        ],
        compiler_params=pltpu.CompilerParams(vmem_limit_bytes=vmem_bytes),
        name="split_heads",
    )(*arrays)


def split_queries_kernel(source, *refs):
    outs, held, come = refs[:4], refs[4], refs[5]
    steps = come.shape[0]
    wide = held.shape[1] // steps
    copies = []
    for step in range(steps):
        lanes = pl.ds(step * wide, wide)
        copy = pltpu.make_async_copy(source.at[:, lanes], held.at[:, lanes], come.at[step])
        copy.start()
        copies.append(copy)
    for copy in copies:
        copy.wait()
    me = lax.axis_index("head")
    for ry, out_ref in enumerate(outs):
        for place in range(out_ref.shape[0]):
            head = me ^ (8 * (place // 2) + 2 * ry + place % 2)
            first = pl.multiple_of(head * HEAD_DIM, HEAD_DIM)
            out_ref[place] = held[:, pl.ds(first, HEAD_DIM)]


def split_queries(array):
    rows, width = array.shape
    shape = jax.ShapeDtypeStruct((width // HEAD_DIM // 4, rows, HEAD_DIM), jnp.bfloat16)
    return pl.pallas_call(
        split_queries_kernel,
        in_specs=[pl.BlockSpec(memory_space=pltpu.HBM)],
        out_specs=[pl.BlockSpec(memory_space=pltpu.VMEM)] * 4,
        out_shape=[shape] * 4,
        scratch_shapes=[pltpu.VMEM((rows, width), jnp.bfloat16), pltpu.SemaphoreType.DMA((4,))],
        compiler_params=pltpu.CompilerParams(vmem_limit_bytes=SMALL_BYTES),
        name="split_queries",
    )(array)


def pack_chips_kernel(*refs):
    *by_y, out_ref = refs
    me = lax.axis_index("head")
    for rz in range(4):
        for core in range(2):
            spot = (me // 8 ^ rz) * 2 + (me % 2 ^ core)
            for ry, source in enumerate(by_y):
                out_ref[spot, ry] = source[2 * rz + core]


def pack_chips(arrays):
    vmem = pl.BlockSpec(memory_space=pltpu.VMEM)
    return pl.pallas_call(
        pack_chips_kernel,
        in_specs=[vmem] * len(arrays),
        out_specs=vmem,
        out_shape=jax.ShapeDtypeStruct((8, len(arrays), *arrays[0].shape[1:]), jnp.bfloat16),
        compiler_params=pltpu.CompilerParams(vmem_limit_bytes=SMALL_BYTES),
        name="pack_chips",
    )(*arrays)


def from_head(array, flip):
    count = lax.axis_size("head")
    return lax.ppermute(array, "head", [(low, low ^ flip) for low in range(count)])


def gather_queries(array):
    near, *others = split_queries(array)
    by_y = [near] + [from_head(part, 2 * ry) for ry, part in zip(range(1, 4), others)]
    groups = [[z * 8 + 2 * y + core for z in range(4) for core in range(2)] for y in range(4)]
    return lax.all_to_all(
        pack_chips(by_y),
        "head",
        split_axis=0,
        concat_axis=0,
        tiled=True,
        axis_index_groups=groups,
    )


def join_heads_kernel(source, out_ref):
    heads, _, _ = source.shape
    for head in range(heads):
        out_ref[:, head * HEAD_DIM : (head + 1) * HEAD_DIM] = source[head]


def join_heads(array):
    heads, rows, _ = array.shape
    return pl.pallas_call(
        join_heads_kernel,
        in_specs=[pl.BlockSpec(memory_space=pltpu.VMEM)],
        out_specs=pl.BlockSpec(memory_space=pltpu.VMEM),
        out_shape=jax.ShapeDtypeStruct((rows, heads * HEAD_DIM), jnp.bfloat16),
        compiler_params=pltpu.CompilerParams(vmem_limit_bytes=SMALL_BYTES),
        name="join_heads",
    )(array)


def pick_kernel(block_select, own_ref, *outs):
    shot = lax.axis_index("shot")
    piece = own_ref.shape[1] // 2
    group = BLK // piece
    for round_index, out_ref in enumerate(outs):
        partner = shot ^ (SHOTS >> (round_index + 1))
        for pick in range(SEL):
            first = block_select[round_index, partner, pick] * group
            out_ref[pick * group : (pick + 1) * group] = own_ref[pl.ds(first, group)]


def pick_blocks(block_select, own):
    shape = jax.ShapeDtypeStruct((FAR // (own.shape[1] // 2),) + own.shape[1:], jnp.bfloat16)
    return pl.pallas_call(
        pick_kernel,
        in_specs=[
            pl.BlockSpec(memory_space=pltpu.SMEM),
            pl.BlockSpec(memory_space=pltpu.VMEM),
        ],
        out_specs=[pl.BlockSpec(memory_space=pltpu.VMEM)] * ROUNDS,
        out_shape=[shape] * ROUNDS,
        compiler_params=pltpu.CompilerParams(vmem_limit_bytes=SMALL_BYTES),
        name="pick_blocks",
    )(block_select, own)


def attend_kernel(lengths, links, own_ref, *refs):
    query_ref, far_refs, out_ref = refs[0], refs[1:-1], refs[-1]
    shot, me = lax.axis_index("shot"), lax.axis_index("head")
    length = lengths[shot]
    _, held, piece, _ = query_ref.shape
    count = SUB // piece
    group = BLK // piece
    blocks = []
    for block in range(LMAX // BLK):
        live = None if (block + 1) * BLK <= LMIN else block * BLK < length
        blocks.append((own_ref, block * group, live))
    for round_index, far_ref in enumerate(far_refs):
        for pick in range(SEL):
            blocks.append((far_ref, pick * group, links[round_index, shot] > 0))
    chunks = [blocks[n : n + CHUNK // BLK] for n in range(0, len(blocks), CHUNK // BLK)]

    def keys_of(chunk):
        parts = []
        for source, first, live in chunk:
            part = source[first : first + group, 0:piece, :].reshape(BLK, HEAD_DIM)
            if live is not None:
                part = jnp.where(live, part, own_ref[0:group, 0:piece, :].reshape(BLK, HEAD_DIM))
            parts.append(part)
        key = jnp.concatenate(parts, axis=0)
        return jnp.concatenate([key, key], axis=1)

    def values_of(chunk):
        parts = []
        for source, first, live in chunk:
            part = source[first : first + group, piece : 2 * piece, :].reshape(BLK, HEAD_DIM)
            part = jnp.concatenate([part, jnp.ones_like(part)], axis=1)
            parts.append(part if live is None else jnp.where(live, part, jnp.zeros_like(part)))
        return jnp.concatenate(parts, axis=0)

    parts = LMAX // SUB
    scores, row_max = None, None
    for part in range(parts + 1):
        new_scores, top, weighted = [], None, None
        if part < parts:
            chip, first = part * count // held, part * count % held
            scaled = query_ref[chip, first : first + count].reshape(SUB, HEAD_DIM).astype(jnp.float32) * FACTOR
            high = scaled.astype(jnp.bfloat16)
            low = (scaled - high.astype(jnp.float32)).astype(jnp.bfloat16)
            query = jnp.concatenate([high, low], axis=1)
        for number, chunk in enumerate(chunks):
            if part < parts:
                score = lax.dot_general(
                    query,
                    keys_of(chunk),
                    (((1,), (1,)), ((), ())),
                    preferred_element_type=jnp.float32,
                )
                new_scores.append(score)
                top = score if top is None else jnp.maximum(top, score)
            if part > 0:
                terms = jnp.exp2(scores[number] - row_max).astype(jnp.bfloat16)
                product = jnp.dot(terms, values_of(chunk), preferred_element_type=jnp.float32)
                weighted = product if weighted is None else weighted + product
        if part > 0:
            result = weighted[:, :HEAD_DIM] / weighted[:, HEAD_DIM : HEAD_DIM + 1]
            for number in range(count):
                chip, place = divmod((part - 1) * count + number, held)
                spot = chip // 2 * 8 + 2 * (me // 2 % held ^ place) + chip % 2
                rows = result[number * piece : (number + 1) * piece]
                rows = jnp.where(spot * piece < length, rows, 0.0)
                out_ref[spot] = rows.astype(jnp.bfloat16)
        if part < parts:
            scores, row_max = new_scores, jnp.max(top, axis=1, keepdims=True)


def attend(lengths, links, own, query, far):
    keys = LMAX + ROUNDS * FAR
    smem = pl.BlockSpec(memory_space=pltpu.SMEM)
    vmem = pl.BlockSpec(memory_space=pltpu.VMEM)
    pieces = own.shape[0], own.shape[1] // 2, HEAD_DIM
    return pl.pallas_call(
        attend_kernel,
        in_specs=[smem, smem] + [vmem] * (2 + ROUNDS),
        out_specs=vmem,
        out_shape=jax.ShapeDtypeStruct(pieces, jnp.bfloat16),
        compiler_params=pltpu.CompilerParams(vmem_limit_bytes=VMEM_BYTES),
        cost_estimate=pl.CostEstimate(
            flops=4 * LMAX * keys * HEAD_DIM, bytes_accessed=2 << 20, transcendentals=LMAX * keys
        ),
        name="attend",
    )(lengths, links, own, query, *far)


def swap(array):
    return lax.all_to_all(array, "head", split_axis=0, concat_axis=0, tiled=True)


def from_partner(array, bit):
    count = lax.axis_size("shot")
    return lax.ppermute(array, "shot", [(low, low ^ bit) for low in range(count)])


def body(queries, key_rows, value_rows, shot_lengths, shot_links, block_select):
    own = swap(split_heads(key_rows[0], value_rows[0], vmem_bytes=LARGE_BYTES))
    query = gather_queries(queries[0])
    far = [
        from_partner(picked, SHOTS >> (round_index + 1))
        for round_index, picked in enumerate(pick_blocks(block_select, own))
    ]
    result = attend(shot_lengths, shot_links, own, query, far)
    return join_heads(swap(result))[None]


def solution(mesh):
    placed = (
        P("shot", "head", None),
        P("shot", "head", None),
        P("shot", "head", None),
        P(),
        P(),
        P(),
    )
    return jax.shard_map(
        body, mesh=mesh, in_specs=placed, out_specs=P("shot", "head", None), check_vma=False
    )
```

```python
import functools

import jax
import jax.numpy as jnp
from jax import lax
from jax.experimental import pallas as pl
from jax.experimental.pallas import tpu as pltpu
from jax.sharding import PartitionSpec as P

HEAD_DIM = 128
LMAX = 2048
LMIN = 1024
BLK = 128
SEL = 2
ROUNDS = 2
SHOTS = 16
FAR = SEL * BLK
FACTOR = HEAD_DIM ** (-0.5) * 1.4426950408889634
CHUNK = 256
SUB = 1024
HEADS_A_STEP = 2
VMEM_BYTES = 46 << 20
SMALL_BYTES = 6 << 20
LARGE_BYTES = 60 << 20


def split_heads_kernel(*refs):
    count = len(refs) - 5
    sources, out_ref, held, made, come, gone = refs[:count], *refs[count:]
    rows = held.shape[1]
    wide = HEADS_A_STEP * HEAD_DIM
    steps = out_ref.shape[0] // HEADS_A_STEP
    arrivals = [
        [
            pltpu.make_async_copy(
                source.at[:, pl.ds(step * wide, wide)],
                held.at[number, :, pl.ds(step * wide, wide)],
                come.at[number, step],
            )
            for number, source in enumerate(sources)
        ]
        for step in range(steps)
    ]
    for step in arrivals:
        for arrival in step:
            arrival.start()
    leaving = []
    for step in range(steps):
        place = pl.ds(step * HEADS_A_STEP, HEADS_A_STEP)
        for number in range(count):
            arrivals[step][number].wait()
            for head in range(step * HEADS_A_STEP, (step + 1) * HEADS_A_STEP):
                made[head, number * rows : (number + 1) * rows, :] = held[
                    number, :, head * HEAD_DIM : (head + 1) * HEAD_DIM
                ]
        copy = pltpu.make_async_copy(made.at[place], out_ref.at[place], gone.at[step])
        copy.start()
        leaving.append(copy)
    for copy in leaving:
        copy.wait()


def split_heads(*arrays, vmem_bytes=SMALL_BYTES):
    count = len(arrays)
    rows, width = arrays[0].shape
    heads = width // HEAD_DIM
    steps = heads // HEADS_A_STEP
    shape = (heads, count * rows, HEAD_DIM)
    return pl.pallas_call(
        split_heads_kernel,
        in_specs=[pl.BlockSpec(memory_space=pltpu.HBM)] * count,
        out_specs=pl.BlockSpec(memory_space=pltpu.HBM),
        out_shape=jax.ShapeDtypeStruct(shape, jnp.bfloat16),
        scratch_shapes=[
            pltpu.VMEM((count, rows, width), jnp.bfloat16),
            pltpu.VMEM(shape, jnp.bfloat16),
            pltpu.SemaphoreType.DMA((count, steps)),
            pltpu.SemaphoreType.DMA((steps,)),
        ],
        compiler_params=pltpu.CompilerParams(vmem_limit_bytes=vmem_bytes),
        name="split_heads",
    )(*arrays)


def split_queries_kernel(source, *refs):
    outs, held, come = refs[:4], refs[4], refs[5]
    steps = come.shape[0]
    wide = held.shape[1] // steps
    copies = []
    for step in range(steps):
        lanes = pl.ds(step * wide, wide)
        copy = pltpu.make_async_copy(source.at[:, lanes], held.at[:, lanes], come.at[step])
        copy.start()
        copies.append(copy)
    for copy in copies:
        copy.wait()
    me = lax.axis_index("head")
    for ry, out_ref in enumerate(outs):
        for place in range(out_ref.shape[0]):
            head = me ^ (8 * (place // 2) + 2 * ry + place % 2)
            first = pl.multiple_of(head * HEAD_DIM, HEAD_DIM)
            out_ref[place] = held[:, pl.ds(first, HEAD_DIM)]


def split_queries(array):
    rows, width = array.shape
    shape = jax.ShapeDtypeStruct((width // HEAD_DIM // 4, rows, HEAD_DIM), jnp.bfloat16)
    return pl.pallas_call(
        split_queries_kernel,
        in_specs=[pl.BlockSpec(memory_space=pltpu.HBM)],
        out_specs=[pl.BlockSpec(memory_space=pltpu.VMEM)] * 4,
        out_shape=[shape] * 4,
        scratch_shapes=[pltpu.VMEM((rows, width), jnp.bfloat16), pltpu.SemaphoreType.DMA((4,))],
        compiler_params=pltpu.CompilerParams(vmem_limit_bytes=SMALL_BYTES),
        name="split_queries",
    )(array)


def pack_chips_kernel(*refs):
    *by_y, out_ref = refs
    me = lax.axis_index("head")
    for rz in range(4):
        for core in range(2):
            spot = (me // 8 ^ rz) * 2 + (me % 2 ^ core)
            for ry, source in enumerate(by_y):
                out_ref[spot, ry] = source[2 * rz + core]


def pack_chips(arrays):
    vmem = pl.BlockSpec(memory_space=pltpu.VMEM)
    return pl.pallas_call(
        pack_chips_kernel,
        in_specs=[vmem] * len(arrays),
        out_specs=vmem,
        out_shape=jax.ShapeDtypeStruct((8, len(arrays), *arrays[0].shape[1:]), jnp.bfloat16),
        compiler_params=pltpu.CompilerParams(vmem_limit_bytes=SMALL_BYTES),
        name="pack_chips",
    )(*arrays)


def from_head(array, flip):
    count = lax.axis_size("head")
    return lax.ppermute(array, "head", [(low, low ^ flip) for low in range(count)])


def gather_queries(array):
    near, *others = split_queries(array)
    by_y = [near] + [from_head(part, 2 * ry) for ry, part in zip(range(1, 4), others)]
    groups = [[z * 8 + 2 * y + core for z in range(4) for core in range(2)] for y in range(4)]
    return lax.all_to_all(
        pack_chips(by_y),
        "head",
        split_axis=0,
        concat_axis=0,
        tiled=True,
        axis_index_groups=groups,
    )


def join_heads_kernel(source, out_ref):
    heads, _, _ = source.shape
    for head in range(heads):
        out_ref[:, head * HEAD_DIM : (head + 1) * HEAD_DIM] = source[head]


def join_heads(array):
    heads, rows, _ = array.shape
    return pl.pallas_call(
        join_heads_kernel,
        in_specs=[pl.BlockSpec(memory_space=pltpu.VMEM)],
        out_specs=pl.BlockSpec(memory_space=pltpu.VMEM),
        out_shape=jax.ShapeDtypeStruct((rows, heads * HEAD_DIM), jnp.bfloat16),
        compiler_params=pltpu.CompilerParams(vmem_limit_bytes=SMALL_BYTES),
        name="join_heads",
    )(array)


def pick_kernel(block_select, own_ref, *outs):
    shot = lax.axis_index("shot")
    piece = own_ref.shape[1] // 2
    group = BLK // piece
    for round_index, out_ref in enumerate(outs):
        partner = shot ^ (SHOTS >> (round_index + 1))
        for pick in range(SEL):
            first = block_select[round_index, partner, pick] * group
            out_ref[pick * group : (pick + 1) * group] = own_ref[pl.ds(first, group)]


def pick_blocks(block_select, own):
    shape = jax.ShapeDtypeStruct((FAR // (own.shape[1] // 2),) + own.shape[1:], jnp.bfloat16)
    return pl.pallas_call(
        pick_kernel,
        in_specs=[
            pl.BlockSpec(memory_space=pltpu.SMEM),
            pl.BlockSpec(memory_space=pltpu.VMEM),
        ],
        out_specs=[pl.BlockSpec(memory_space=pltpu.VMEM)] * ROUNDS,
        out_shape=[shape] * ROUNDS,
        compiler_params=pltpu.CompilerParams(vmem_limit_bytes=SMALL_BYTES),
        name="pick_blocks",
    )(block_select, own)


def attend_kernel(lengths, links, own_ref, *refs):
    query_ref, far_refs, out_ref = refs[0], refs[1:-1], refs[-1]
    shot, me = lax.axis_index("shot"), lax.axis_index("head")
    length = lengths[shot]
    _, held, piece, _ = query_ref.shape
    count = SUB // piece
    group = BLK // piece
    blocks = []
    for block in range(LMAX // BLK):
        live = None if (block + 1) * BLK <= LMIN else block * BLK < length
        blocks.append((own_ref, block * group, live))
    for round_index, far_ref in enumerate(far_refs):
        for pick in range(SEL):
            blocks.append((far_ref, pick * group, links[round_index, shot] > 0))
    chunks = [blocks[n : n + CHUNK // BLK] for n in range(0, len(blocks), CHUNK // BLK)]

    def keys_of(chunk):
        parts = []
        for source, first, live in chunk:
            part = source[first : first + group, 0:piece, :].reshape(BLK, HEAD_DIM)
            if live is not None:
                part = jnp.where(live, part, own_ref[0:group, 0:piece, :].reshape(BLK, HEAD_DIM))
            parts.append(part)
        key = jnp.concatenate(parts, axis=0)
        return jnp.concatenate([key, key], axis=1)

    def values_of(chunk):
        parts = []
        for source, first, live in chunk:
            part = source[first : first + group, piece : 2 * piece, :].reshape(BLK, HEAD_DIM)
            part = jnp.concatenate([part, jnp.ones_like(part)], axis=1)
            parts.append(part if live is None else jnp.where(live, part, jnp.zeros_like(part)))
        return jnp.concatenate(parts, axis=0)

    parts = LMAX // SUB
    scores, row_max = None, None
    for part in range(parts + 1):
        new_scores, top, weighted = [], None, None
        if part < parts:
            chips = slice(part * count // held, (part + 1) * count // held)
            scaled = query_ref[chips].reshape(SUB, HEAD_DIM).astype(jnp.float32) * FACTOR
            high = scaled.astype(jnp.bfloat16)
            low = (scaled - high.astype(jnp.float32)).astype(jnp.bfloat16)
            query = jnp.concatenate([high, low], axis=1)
        for number, chunk in enumerate(chunks):
            if part < parts:
                score = lax.dot_general(
                    query,
                    keys_of(chunk),
                    (((1,), (1,)), ((), ())),
                    preferred_element_type=jnp.float32,
                )
                new_scores.append(score)
                top = score if top is None else jnp.maximum(top, score)
            if part > 0:
                terms = jnp.exp2(scores[number] - row_max).astype(jnp.bfloat16)
                product = jnp.dot(terms, values_of(chunk), preferred_element_type=jnp.float32)
                weighted = product if weighted is None else weighted + product
        if part > 0:
            result = weighted[:, :HEAD_DIM] / weighted[:, HEAD_DIM : HEAD_DIM + 1]
            for number in range(count):
                chip, place = divmod((part - 1) * count + number, held)
                spot = chip // 2 * 8 + 2 * (me // 2 % held ^ place) + chip % 2
                rows = result[number * piece : (number + 1) * piece]
                rows = jnp.where(spot * piece < length, rows, 0.0)
                out_ref[spot] = rows.astype(jnp.bfloat16)
        if part < parts:
            scores, row_max = new_scores, jnp.max(top, axis=1, keepdims=True)


def attend(lengths, links, own, query, far):
    keys = LMAX + ROUNDS * FAR
    smem = pl.BlockSpec(memory_space=pltpu.SMEM)
    vmem = pl.BlockSpec(memory_space=pltpu.VMEM)
    pieces = own.shape[0], own.shape[1] // 2, HEAD_DIM
    return pl.pallas_call(
        attend_kernel,
        in_specs=[smem, smem] + [vmem] * (2 + ROUNDS),
        out_specs=vmem,
        out_shape=jax.ShapeDtypeStruct(pieces, jnp.bfloat16),
        compiler_params=pltpu.CompilerParams(vmem_limit_bytes=VMEM_BYTES),
        cost_estimate=pl.CostEstimate(
            flops=4 * LMAX * keys * HEAD_DIM, bytes_accessed=2 << 20, transcendentals=LMAX * keys
        ),
        name="attend",
    )(lengths, links, own, query, *far)


def swap(array):
    return lax.all_to_all(array, "head", split_axis=0, concat_axis=0, tiled=True)


def from_partner(array, bit):
    count = lax.axis_size("shot")
    return lax.ppermute(array, "shot", [(low, low ^ bit) for low in range(count)])


def body(queries, key_rows, value_rows, shot_lengths, shot_links, block_select):
    own = swap(split_heads(key_rows[0], value_rows[0], vmem_bytes=LARGE_BYTES))
    query = gather_queries(queries[0])
    far = [
        from_partner(picked, SHOTS >> (round_index + 1))
        for round_index, picked in enumerate(pick_blocks(block_select, own))
    ]
    result = attend(shot_lengths, shot_links, own, query, far)
    return join_heads(swap(result))[None]


def solution(mesh):
    placed = (
        P("shot", "head", None),
        P("shot", "head", None),
        P("shot", "head", None),
        P(),
        P(),
        P(),
    )
    return jax.shard_map(
        body, mesh=mesh, in_specs=placed, out_specs=P("shot", "head", None), check_vma=False
    )
```

```python
import functools

import jax
import jax.numpy as jnp
from jax import lax
from jax.experimental import pallas as pl
from jax.experimental.pallas import tpu as pltpu
from jax.sharding import PartitionSpec as P

HEAD_DIM = 128
LMAX = 2048
LMIN = 1024
BLK = 128
SEL = 2
ROUNDS = 2
SHOTS = 16
FAR = SEL * BLK
FACTOR = HEAD_DIM ** (-0.5) * 1.4426950408889634
CHUNK = 256
EARLY = 512
HEADS_A_STEP = 4
VMEM_BYTES = 28 << 20
SMALL_BYTES = 6 << 20
LARGE_BYTES = 60 << 20


def split_heads_kernel(*refs):
    count = len(refs) - 5
    sources, out_ref, held, made, come, gone = refs[:count], *refs[count:]
    rows = held.shape[1]
    wide = HEADS_A_STEP * HEAD_DIM
    steps = out_ref.shape[0] // HEADS_A_STEP
    arrivals = [
        [
            pltpu.make_async_copy(
                source.at[:, pl.ds(step * wide, wide)],
                held.at[number, :, pl.ds(step * wide, wide)],
                come.at[number, step],
            )
            for number, source in enumerate(sources)
        ]
        for step in range(steps)
    ]
    for step in arrivals:
        for arrival in step:
            arrival.start()
    leaving = []
    for step in range(steps):
        place = pl.ds(step * HEADS_A_STEP, HEADS_A_STEP)
        for number in range(count):
            arrivals[step][number].wait()
            for head in range(step * HEADS_A_STEP, (step + 1) * HEADS_A_STEP):
                made[head, number * rows : (number + 1) * rows, :] = held[
                    number, :, head * HEAD_DIM : (head + 1) * HEAD_DIM
                ]
        copy = pltpu.make_async_copy(made.at[place], out_ref.at[place], gone.at[step])
        copy.start()
        leaving.append(copy)
    for copy in leaving:
        copy.wait()


def split_heads(*arrays, vmem_bytes=SMALL_BYTES):
    count = len(arrays)
    rows, width = arrays[0].shape
    heads = width // HEAD_DIM
    steps = heads // HEADS_A_STEP
    shape = (heads, count * rows, HEAD_DIM)
    return pl.pallas_call(
        split_heads_kernel,
        in_specs=[pl.BlockSpec(memory_space=pltpu.HBM)] * count,
        out_specs=pl.BlockSpec(memory_space=pltpu.HBM),
        out_shape=jax.ShapeDtypeStruct(shape, jnp.bfloat16),
        scratch_shapes=[
            pltpu.VMEM((count, rows, width), jnp.bfloat16),
            pltpu.VMEM(shape, jnp.bfloat16),
            pltpu.SemaphoreType.DMA((count, steps)),
            pltpu.SemaphoreType.DMA((steps,)),
        ],
        compiler_params=pltpu.CompilerParams(vmem_limit_bytes=vmem_bytes),
        name="split_heads",
    )(*arrays)


def split_queries_kernel(source, *refs):
    outs, held, come = refs[:4], refs[4], refs[5]
    steps = come.shape[0]
    wide = held.shape[1] // steps
    copies = []
    for step in range(steps):
        lanes = pl.ds(step * wide, wide)
        copy = pltpu.make_async_copy(source.at[:, lanes], held.at[:, lanes], come.at[step])
        copy.start()
        copies.append(copy)
    for copy in copies:
        copy.wait()
    me = lax.axis_index("head")
    for ry, out_ref in enumerate(outs):
        for place in range(out_ref.shape[0]):
            head = me ^ (8 * (place // 2) + 2 * ry + place % 2)
            first = pl.multiple_of(head * HEAD_DIM, HEAD_DIM)
            out_ref[place] = held[:, pl.ds(first, HEAD_DIM)]


def split_queries(array):
    rows, width = array.shape
    shape = jax.ShapeDtypeStruct((width // HEAD_DIM // 4, rows, HEAD_DIM), jnp.bfloat16)
    return pl.pallas_call(
        split_queries_kernel,
        in_specs=[pl.BlockSpec(memory_space=pltpu.HBM)],
        out_specs=[pl.BlockSpec(memory_space=pltpu.VMEM)] * 4,
        out_shape=[shape] * 4,
        scratch_shapes=[pltpu.VMEM((rows, width), jnp.bfloat16), pltpu.SemaphoreType.DMA((4,))],
        compiler_params=pltpu.CompilerParams(vmem_limit_bytes=SMALL_BYTES),
        name="split_queries",
    )(array)


def pack_kernel(*refs, plan):
    sources, outs = refs[: len(refs) - len(plan)], refs[len(refs) - len(plan) :]
    for out_ref, pieces in zip(outs, plan):
        for place, (number, piece) in enumerate(pieces):
            out_ref[place] = sources[number][piece]


def pack(arrays, plan):
    vmem = pl.BlockSpec(memory_space=pltpu.VMEM)
    return pl.pallas_call(
        functools.partial(pack_kernel, plan=plan),
        in_specs=[vmem] * len(arrays),
        out_specs=[vmem] * len(plan),
        out_shape=[
            jax.ShapeDtypeStruct((len(pieces),) + arrays[0].shape[1:], jnp.bfloat16)
            for pieces in plan
        ],
        compiler_params=pltpu.CompilerParams(vmem_limit_bytes=SMALL_BYTES),
        name="pack",
    )(*arrays)


def pack_chips_kernel(*refs):
    *by_y, out_ref = refs
    me = lax.axis_index("head")
    for rz in range(4):
        for core in range(2):
            spot = (me // 8 ^ rz) * 2 + (me % 2 ^ core)
            for ry, source in enumerate(by_y):
                out_ref[spot, ry] = source[2 * rz + core]


def pack_chips(arrays):
    vmem = pl.BlockSpec(memory_space=pltpu.VMEM)
    return pl.pallas_call(
        pack_chips_kernel,
        in_specs=[vmem] * len(arrays),
        out_specs=vmem,
        out_shape=jax.ShapeDtypeStruct((8, len(arrays), *arrays[0].shape[1:]), jnp.bfloat16),
        compiler_params=pltpu.CompilerParams(vmem_limit_bytes=SMALL_BYTES),
        name="pack_chips",
    )(*arrays)


def from_head(array, flip):
    count = lax.axis_size("head")
    return lax.ppermute(array, "head", [(low, low ^ flip) for low in range(count)])


def gather_queries(array):
    near, *others = split_queries(array)
    by_y = [near] + [from_head(part, 2 * ry) for ry, part in zip(range(1, 4), others)]
    groups = [[z * 8 + 2 * y + core for z in range(4) for core in range(2)] for y in range(4)]
    keep, send = pack(by_y, [[(ry, core) for ry in range(4)] for core in range(2)])
    rest = lax.all_to_all(
        pack_chips(by_y),
        "head",
        split_axis=0,
        concat_axis=0,
        tiled=True,
        axis_index_groups=groups,
    )
    return keep, from_head(send, 1), rest


def join_heads_kernel(source, out_ref):
    heads, _, _ = source.shape
    for head in range(heads):
        out_ref[:, head * HEAD_DIM : (head + 1) * HEAD_DIM] = source[head]


def join_heads(array):
    heads, rows, _ = array.shape
    return pl.pallas_call(
        join_heads_kernel,
        in_specs=[pl.BlockSpec(memory_space=pltpu.VMEM)],
        out_specs=pl.BlockSpec(memory_space=pltpu.VMEM),
        out_shape=jax.ShapeDtypeStruct((rows, heads * HEAD_DIM), jnp.bfloat16),
        compiler_params=pltpu.CompilerParams(vmem_limit_bytes=SMALL_BYTES),
        name="join_heads",
    )(array)


def pick_kernel(block_select, own_ref, *outs):
    shot = lax.axis_index("shot")
    piece = own_ref.shape[1] // 2
    group = BLK // piece
    for round_index, out_ref in enumerate(outs):
        partner = shot ^ (SHOTS >> (round_index + 1))
        for pick in range(SEL):
            first = block_select[round_index, partner, pick] * group
            out_ref[pick * group : (pick + 1) * group] = own_ref[pl.ds(first, group)]


def pick_blocks(block_select, own):
    shape = jax.ShapeDtypeStruct((FAR // (own.shape[1] // 2),) + own.shape[1:], jnp.bfloat16)
    return pl.pallas_call(
        pick_kernel,
        in_specs=[
            pl.BlockSpec(memory_space=pltpu.SMEM),
            pl.BlockSpec(memory_space=pltpu.VMEM),
        ],
        out_specs=[pl.BlockSpec(memory_space=pltpu.VMEM)] * ROUNDS,
        out_shape=[shape] * ROUNDS,
        compiler_params=pltpu.CompilerParams(vmem_limit_bytes=SMALL_BYTES),
        name="pick_blocks",
    )(block_select, own)


def keys_of(blocks, piece, spare):
    parts = []
    for source, first, live in blocks:
        place = slice(first, first + BLK // piece)
        part = source[place, 0:piece, :].reshape(BLK, HEAD_DIM)
        if live is not None:
            part = jnp.where(live, part, spare[0 : BLK // piece, 0:piece, :].reshape(BLK, HEAD_DIM))
        parts.append(part)
    key = jnp.concatenate(parts, axis=0)
    return jnp.concatenate([key, key], axis=1)


def values_of(blocks, piece):
    parts = []
    for source, first, live in blocks:
        place = slice(first, first + BLK // piece)
        part = source[place, piece : 2 * piece, :].reshape(BLK, HEAD_DIM)
        part = jnp.concatenate([part, jnp.ones_like(part)], axis=1)
        parts.append(part if live is None else jnp.where(live, part, jnp.zeros_like(part)))
    return jnp.concatenate(parts, axis=0)


def own_blocks(own_ref, piece, length):
    blocks = []
    for block in range(LMAX // BLK):
        live = None if (block + 1) * BLK <= LMIN else block * BLK < length
        blocks.append((own_ref, block * (BLK // piece), live))
    return blocks


def attend_items(items, piece, spare):
    per_chunk = CHUNK // BLK
    scores, row_max, before = [], None, None
    for item in items + [None]:
        new_scores, top, weighted, chunks = [], None, None, []
        if item is not None:
            queries, blocks, floor, _ = item
            scaled = queries().astype(jnp.float32) * FACTOR
            high = scaled.astype(jnp.bfloat16)
            low = (scaled - high.astype(jnp.float32)).astype(jnp.bfloat16)
            query = jnp.concatenate([high, low], axis=1)
            chunks = [blocks[n : n + per_chunk] for n in range(0, len(blocks), per_chunk)]
        for number in range(max(len(chunks), len(scores))):
            if number < len(chunks):
                score = lax.dot_general(
                    query,
                    keys_of(chunks[number], piece, spare),
                    (((1,), (1,)), ((), ())),
                    preferred_element_type=jnp.float32,
                )
                new_scores.append(score)
                top = score if top is None else jnp.maximum(top, score)
            if number < len(scores):
                terms = jnp.exp2(scores[number] - row_max).astype(jnp.bfloat16)
                product = jnp.dot(
                    terms, values_of(before[0][number], piece), preferred_element_type=jnp.float32
                )
                weighted = product if weighted is None else weighted + product
        if before is not None:
            before[1](weighted, row_max)
        if item is not None:
            scores, row_max = new_scores, floor(jnp.max(top, axis=1, keepdims=True))
            before = (chunks, item[3])


def early_queries(keep_ref, come_ref):
    both = jnp.concatenate([keep_ref[...], come_ref[...]], axis=0)
    return both.reshape(EARLY, HEAD_DIM)


def attend_early_kernel(lengths, links, own_ref, keep_ref, come_ref, sum_ref, max_ref):
    piece = own_ref.shape[1] // 2
    blocks = own_blocks(own_ref, piece, lengths[lax.axis_index("shot")])

    def item(source, place):
        def finish(weighted, row_max):
            sum_ref[place, :] = weighted
            max_ref[place, :] = jnp.broadcast_to(row_max, (weighted.shape[0], HEAD_DIM))

        def queries():
            return source[...].reshape(EARLY // 2, HEAD_DIM)

        return queries, blocks, lambda top: top, finish

    halves = slice(0, EARLY // 2), slice(EARLY // 2, EARLY)
    items = [item(source, place) for source, place in zip((keep_ref, come_ref), halves)]
    attend_items(items, piece, own_ref)


def attend_late_kernel(lengths, links, own_ref, query_ref, keep_ref, come_ref, *refs):
    sum_ref, max_ref, *far_refs, out_ref = refs
    shot, me = lax.axis_index("shot"), lax.axis_index("head")
    length = lengths[shot]
    piece = own_ref.shape[1] // 2
    far = []
    for round_index, far_ref in enumerate(far_refs):
        for pick in range(SEL):
            far.append((far_ref, pick * (BLK // piece), links[round_index, shot] > 0))
    every = own_blocks(own_ref, piece, length) + far

    def store(weighted, spots):
        result = weighted[:, :HEAD_DIM] / weighted[:, HEAD_DIM : HEAD_DIM + 1]
        for number, spot in enumerate(spots):
            rows = result[number * piece : (number + 1) * piece]
            out_ref[spot] = jnp.where(spot * piece < length, rows, 0.0).astype(jnp.bfloat16)

    def finish_early(weighted, row_max):
        kept = jnp.exp2(max_ref[...] - row_max)
        kept = sum_ref[...] * jnp.concatenate([kept, kept], axis=1)
        store(weighted + kept, [me ^ (2 * ry + core) for core in range(2) for ry in range(4)])

    def late_item(chips):
        spots = [
            (me // 8 ^ rz) * 8 + 2 * (me // 2 % 4 ^ k) + core for rz, core in chips for k in range(4)
        ]

        def queries():
            loads = [query_ref[(me // 8 ^ rz) * 2 + core] for rz, core in chips]
            return jnp.concatenate(loads, axis=0).reshape(len(spots) * piece, HEAD_DIM)

        return queries, every, lambda top: top, lambda weighted, _: store(weighted, spots)

    early = (
        functools.partial(early_queries, keep_ref, come_ref),
        far,
        lambda top: jnp.maximum(top, max_ref[:, 0:1]),
        finish_early,
    )
    chips = [(rz, core) for rz in range(1, 4) for core in range(2)]
    attend_items([early, late_item(chips[:3]), late_item(chips[3:])], piece, own_ref)


def attend_cost(queries, keys):
    return pl.CostEstimate(
        flops=4 * queries * keys * HEAD_DIM,
        bytes_accessed=2 << 20,
        transcendentals=queries * keys,
    )


def attend_early(lengths, links, own, keep, come):
    smem, vmem = pl.BlockSpec(memory_space=pltpu.SMEM), pl.BlockSpec(memory_space=pltpu.VMEM)
    return pl.pallas_call(
        attend_early_kernel,
        in_specs=[smem, smem] + [vmem] * 3,
        out_specs=[vmem] * 2,
        out_shape=[
            jax.ShapeDtypeStruct((EARLY, 2 * HEAD_DIM), jnp.float32),
            jax.ShapeDtypeStruct((EARLY, HEAD_DIM), jnp.float32),
        ],
        compiler_params=pltpu.CompilerParams(vmem_limit_bytes=12 << 20),
        cost_estimate=attend_cost(EARLY, LMAX),
        name="attend_early",
    )(lengths, links, own, keep, come)


def attend_late(lengths, links, own, rest, keep, come, sums, tops, far):
    smem, vmem = pl.BlockSpec(memory_space=pltpu.SMEM), pl.BlockSpec(memory_space=pltpu.VMEM)
    shape = (own.shape[0], own.shape[1] // 2, HEAD_DIM)
    return pl.pallas_call(
        attend_late_kernel,
        in_specs=[smem, smem] + [vmem] * (6 + ROUNDS),
        out_specs=vmem,
        out_shape=jax.ShapeDtypeStruct(shape, jnp.bfloat16),
        compiler_params=pltpu.CompilerParams(vmem_limit_bytes=VMEM_BYTES),
        cost_estimate=attend_cost(LMAX - EARLY, LMAX + ROUNDS * FAR),
        name="attend_late",
    )(lengths, links, own, rest, keep, come, sums, tops, *far)


def swap(array):
    return lax.all_to_all(array, "head", split_axis=0, concat_axis=0, tiled=True)


def from_partner(array, bit):
    count = lax.axis_size("shot")
    return lax.ppermute(array, "shot", [(low, low ^ bit) for low in range(count)])


def body(queries, key_rows, value_rows, shot_lengths, shot_links, block_select):
    own = swap(split_heads(key_rows[0], value_rows[0], vmem_bytes=LARGE_BYTES))
    keep, come, rest = gather_queries(queries[0])
    far = [
        from_partner(picked, SHOTS >> (round_index + 1))
        for round_index, picked in enumerate(pick_blocks(block_select, own))
    ]
    sums, tops = attend_early(shot_lengths, shot_links, own, keep, come)
    result = attend_late(shot_lengths, shot_links, own, rest, keep, come, sums, tops, far)
    return join_heads(swap(result))[None]


def solution(mesh):
    placed = (
        P("shot", "head", None),
        P("shot", "head", None),
        P("shot", "head", None),
        P(),
        P(),
        P(),
    )
    return jax.shard_map(
        body, mesh=mesh, in_specs=placed, out_specs=P("shot", "head", None), check_vma=False
    )
```

```python
import functools

import jax
import jax.numpy as jnp
from jax import lax
from jax.experimental import pallas as pl
from jax.experimental.pallas import tpu as pltpu
from jax.sharding import PartitionSpec as P

HEAD_DIM = 128
LMAX = 2048
LMIN = 1024
BLK = 128
SEL = 2
ROUNDS = 2
SHOTS = 16
FAR = SEL * BLK
FACTOR = HEAD_DIM ** (-0.5) * 1.4426950408889634
CHUNK = 256
EARLY = 512
HEADS_A_STEP = 4
VMEM_BYTES = 28 << 20
SMALL_BYTES = 6 << 20
LARGE_BYTES = 60 << 20


def split_heads_kernel(*refs):
    count = len(refs) - 5
    sources, out_ref, held, made, come, gone = refs[:count], *refs[count:]
    rows = held.shape[1]
    wide = HEADS_A_STEP * HEAD_DIM
    steps = out_ref.shape[0] // HEADS_A_STEP
    arrivals = [
        [
            pltpu.make_async_copy(
                source.at[:, pl.ds(step * wide, wide)],
                held.at[number, :, pl.ds(step * wide, wide)],
                come.at[number, step],
            )
            for number, source in enumerate(sources)
        ]
        for step in range(steps)
    ]
    for step in arrivals:
        for arrival in step:
            arrival.start()
    leaving = []
    for step in range(steps):
        place = pl.ds(step * HEADS_A_STEP, HEADS_A_STEP)
        for number in range(count):
            arrivals[step][number].wait()
            for head in range(step * HEADS_A_STEP, (step + 1) * HEADS_A_STEP):
                made[head, number * rows : (number + 1) * rows, :] = held[
                    number, :, head * HEAD_DIM : (head + 1) * HEAD_DIM
                ]
        copy = pltpu.make_async_copy(made.at[place], out_ref.at[place], gone.at[step])
        copy.start()
        leaving.append(copy)
    for copy in leaving:
        copy.wait()


def split_heads(*arrays, vmem_bytes=SMALL_BYTES):
    count = len(arrays)
    rows, width = arrays[0].shape
    heads = width // HEAD_DIM
    steps = heads // HEADS_A_STEP
    shape = (heads, count * rows, HEAD_DIM)
    return pl.pallas_call(
        split_heads_kernel,
        in_specs=[pl.BlockSpec(memory_space=pltpu.HBM)] * count,
        out_specs=pl.BlockSpec(memory_space=pltpu.HBM),
        out_shape=jax.ShapeDtypeStruct(shape, jnp.bfloat16),
        scratch_shapes=[
            pltpu.VMEM((count, rows, width), jnp.bfloat16),
            pltpu.VMEM(shape, jnp.bfloat16),
            pltpu.SemaphoreType.DMA((count, steps)),
            pltpu.SemaphoreType.DMA((steps,)),
        ],
        compiler_params=pltpu.CompilerParams(vmem_limit_bytes=vmem_bytes),
        name="split_heads",
    )(*arrays)


def split_queries_kernel(source, *refs):
    outs, held, come = refs[:4], refs[4], refs[5]
    steps = come.shape[0]
    wide = held.shape[1] // steps
    copies = []
    for step in range(steps):
        lanes = pl.ds(step * wide, wide)
        copy = pltpu.make_async_copy(source.at[:, lanes], held.at[:, lanes], come.at[step])
        copy.start()
        copies.append(copy)
    for copy in copies:
        copy.wait()
    me = lax.axis_index("head")
    for ry, out_ref in enumerate(outs):
        for place in range(out_ref.shape[0]):
            head = me ^ (8 * (place // 2) + 2 * ry + place % 2)
            first = pl.multiple_of(head * HEAD_DIM, HEAD_DIM)
            out_ref[place] = held[:, pl.ds(first, HEAD_DIM)]


def split_queries(array):
    rows, width = array.shape
    shape = jax.ShapeDtypeStruct((width // HEAD_DIM // 4, rows, HEAD_DIM), jnp.bfloat16)
    return pl.pallas_call(
        split_queries_kernel,
        in_specs=[pl.BlockSpec(memory_space=pltpu.HBM)],
        out_specs=[pl.BlockSpec(memory_space=pltpu.VMEM)] * 4,
        out_shape=[shape] * 4,
        scratch_shapes=[pltpu.VMEM((rows, width), jnp.bfloat16), pltpu.SemaphoreType.DMA((4,))],
        compiler_params=pltpu.CompilerParams(vmem_limit_bytes=SMALL_BYTES),
        name="split_queries",
    )(array)


def pack_kernel(*refs, plan):
    sources, outs = refs[: len(refs) - len(plan)], refs[len(refs) - len(plan) :]
    for out_ref, pieces in zip(outs, plan):
        for place, (number, piece) in enumerate(pieces):
            out_ref[place] = sources[number][piece]


def pack(arrays, plan):
    vmem = pl.BlockSpec(memory_space=pltpu.VMEM)
    return pl.pallas_call(
        functools.partial(pack_kernel, plan=plan),
        in_specs=[vmem] * len(arrays),
        out_specs=[vmem] * len(plan),
        out_shape=[
            jax.ShapeDtypeStruct((len(pieces),) + arrays[0].shape[1:], jnp.bfloat16)
            for pieces in plan
        ],
        compiler_params=pltpu.CompilerParams(vmem_limit_bytes=SMALL_BYTES),
        name="pack",
    )(*arrays)


def pack_chips_kernel(*refs):
    *by_y, out_ref = refs
    me = lax.axis_index("head")
    for rz in range(4):
        for core in range(2):
            spot = (me // 8 ^ rz) * 2 + (me % 2 ^ core)
            for ry, source in enumerate(by_y):
                out_ref[spot, ry] = source[2 * rz + core]


def pack_chips(arrays):
    vmem = pl.BlockSpec(memory_space=pltpu.VMEM)
    return pl.pallas_call(
        pack_chips_kernel,
        in_specs=[vmem] * len(arrays),
        out_specs=vmem,
        out_shape=jax.ShapeDtypeStruct((8, len(arrays), *arrays[0].shape[1:]), jnp.bfloat16),
        compiler_params=pltpu.CompilerParams(vmem_limit_bytes=SMALL_BYTES),
        name="pack_chips",
    )(*arrays)


def from_head(array, flip):
    count = lax.axis_size("head")
    return lax.ppermute(array, "head", [(low, low ^ flip) for low in range(count)])


def gather_queries(array):
    near, *others = split_queries(array)
    by_y = [near] + [from_head(part, 2 * ry) for ry, part in zip(range(1, 4), others)]
    groups = [[z * 8 + 2 * y + core for z in range(4) for core in range(2)] for y in range(4)]
    keep, send = pack(by_y, [[(ry, core) for ry in range(4)] for core in range(2)])
    rest = lax.all_to_all(
        pack_chips(by_y),
        "head",
        split_axis=0,
        concat_axis=0,
        tiled=True,
        axis_index_groups=groups,
    )
    return keep, from_head(send, 1), rest


def join_heads_kernel(source, out_ref):
    heads, _, _ = source.shape
    for head in range(heads):
        out_ref[:, head * HEAD_DIM : (head + 1) * HEAD_DIM] = source[head]


def join_heads(array):
    heads, rows, _ = array.shape
    return pl.pallas_call(
        join_heads_kernel,
        in_specs=[pl.BlockSpec(memory_space=pltpu.VMEM)],
        out_specs=pl.BlockSpec(memory_space=pltpu.VMEM),
        out_shape=jax.ShapeDtypeStruct((rows, heads * HEAD_DIM), jnp.bfloat16),
        compiler_params=pltpu.CompilerParams(vmem_limit_bytes=SMALL_BYTES),
        name="join_heads",
    )(array)


def pick_kernel(block_select, own_ref, *outs):
    shot = lax.axis_index("shot")
    piece = own_ref.shape[1] // 2
    group = BLK // piece
    for round_index, out_ref in enumerate(outs):
        partner = shot ^ (SHOTS >> (round_index + 1))
        for pick in range(SEL):
            first = block_select[round_index, partner, pick] * group
            out_ref[pick * group : (pick + 1) * group] = own_ref[pl.ds(first, group)]


def pick_blocks(block_select, own):
    shape = jax.ShapeDtypeStruct((FAR // (own.shape[1] // 2),) + own.shape[1:], jnp.bfloat16)
    return pl.pallas_call(
        pick_kernel,
        in_specs=[
            pl.BlockSpec(memory_space=pltpu.SMEM),
            pl.BlockSpec(memory_space=pltpu.VMEM),
        ],
        out_specs=[pl.BlockSpec(memory_space=pltpu.VMEM)] * ROUNDS,
        out_shape=[shape] * ROUNDS,
        compiler_params=pltpu.CompilerParams(vmem_limit_bytes=SMALL_BYTES),
        name="pick_blocks",
    )(block_select, own)


def keys_of(blocks, piece, spare):
    parts = []
    for source, first, live in blocks:
        place = slice(first, first + BLK // piece)
        part = source[place, 0:piece, :].reshape(BLK, HEAD_DIM)
        if live is not None:
            part = jnp.where(live, part, spare[0 : BLK // piece, 0:piece, :].reshape(BLK, HEAD_DIM))
        parts.append(part)
    key = jnp.concatenate(parts, axis=0)
    return jnp.concatenate([key, key], axis=1)


def values_of(blocks, piece):
    parts = []
    for source, first, live in blocks:
        place = slice(first, first + BLK // piece)
        part = source[place, piece : 2 * piece, :].reshape(BLK, HEAD_DIM)
        part = jnp.concatenate([part, jnp.ones_like(part)], axis=1)
        parts.append(part if live is None else jnp.where(live, part, jnp.zeros_like(part)))
    return jnp.concatenate(parts, axis=0)


def own_blocks(own_ref, piece, length):
    blocks = []
    for block in range(LMAX // BLK):
        live = None if (block + 1) * BLK <= LMIN else block * BLK < length
        blocks.append((own_ref, block * (BLK // piece), live))
    return blocks


def attend_items(items, piece, spare):
    per_chunk = CHUNK // BLK
    scores, row_max, before = [], None, None
    for item in items + [None]:
        new_scores, top, weighted, chunks = [], None, None, []
        if item is not None:
            queries, blocks, floor, _ = item
            scaled = queries().astype(jnp.float32) * FACTOR
            high = scaled.astype(jnp.bfloat16)
            low = (scaled - high.astype(jnp.float32)).astype(jnp.bfloat16)
            query = jnp.concatenate([high, low], axis=1)
            chunks = [blocks[n : n + per_chunk] for n in range(0, len(blocks), per_chunk)]
        for number in range(max(len(chunks), len(scores))):
            if number < len(chunks):
                score = lax.dot_general(
                    query,
                    keys_of(chunks[number], piece, spare),
                    (((1,), (1,)), ((), ())),
                    preferred_element_type=jnp.float32,
                )
                new_scores.append(score)
                top = score if top is None else jnp.maximum(top, score)
            if number < len(scores):
                terms = jnp.exp2(scores[number] - row_max).astype(jnp.bfloat16)
                product = jnp.dot(
                    terms, values_of(before[0][number], piece), preferred_element_type=jnp.float32
                )
                weighted = product if weighted is None else weighted + product
        if before is not None:
            before[1](weighted, row_max)
        if item is not None:
            scores, row_max = new_scores, floor(jnp.max(top, axis=1, keepdims=True))
            before = (chunks, item[3])


def early_queries(keep_ref, come_ref):
    both = jnp.concatenate([keep_ref[...], come_ref[...]], axis=0)
    return both.reshape(EARLY, HEAD_DIM)


def attend_early_kernel(lengths, links, own_ref, keep_ref, come_ref, sum_ref, max_ref):
    piece = own_ref.shape[1] // 2
    blocks = own_blocks(own_ref, piece, lengths[lax.axis_index("shot")])

    def item(source, place):
        def finish(weighted, row_max):
            sum_ref[place, :] = weighted
            max_ref[place, :] = jnp.broadcast_to(row_max, (weighted.shape[0], HEAD_DIM))

        def queries():
            return source[...].reshape(EARLY // 2, HEAD_DIM)

        return queries, blocks, lambda top: top, finish

    halves = slice(0, EARLY // 2), slice(EARLY // 2, EARLY)
    items = [item(source, place) for source, place in zip((keep_ref, come_ref), halves)]
    attend_items(items, piece, own_ref)


def attend_late_kernel(lengths, links, own_ref, query_ref, keep_ref, come_ref, *refs):
    sum_ref, max_ref, *far_refs, out_ref = refs
    shot, me = lax.axis_index("shot"), lax.axis_index("head")
    length = lengths[shot]
    piece = own_ref.shape[1] // 2
    far = []
    for round_index, far_ref in enumerate(far_refs):
        for pick in range(SEL):
            far.append((far_ref, pick * (BLK // piece), links[round_index, shot] > 0))
    every = own_blocks(own_ref, piece, length) + far

    def store(weighted, spots):
        result = weighted[:, :HEAD_DIM] / weighted[:, HEAD_DIM : HEAD_DIM + 1]
        for number, spot in enumerate(spots):
            rows = result[number * piece : (number + 1) * piece]
            out_ref[spot] = jnp.where(spot * piece < length, rows, 0.0).astype(jnp.bfloat16)

    def finish_early(weighted, row_max):
        kept = jnp.exp2(max_ref[...] - row_max)
        kept = sum_ref[...] * jnp.concatenate([kept, kept], axis=1)
        store(weighted + kept, [me ^ (2 * ry + core) for core in range(2) for ry in range(4)])

    def late_item(chips):
        spots = [
            (me // 8 ^ rz) * 8 + 2 * (me // 2 % 4 ^ k) + core for rz, core in chips for k in range(4)
        ]

        def queries():
            loads = [query_ref[(me // 8 ^ rz) * 2 + core] for rz, core in chips]
            return jnp.concatenate(loads, axis=0).reshape(len(spots) * piece, HEAD_DIM)

        return queries, every, lambda top: top, lambda weighted, _: store(weighted, spots)

    early = (
        functools.partial(early_queries, keep_ref, come_ref),
        far,
        lambda top: jnp.maximum(top, max_ref[:, 0:1]),
        finish_early,
    )
    chips = [(rz, core) for rz in range(1, 4) for core in range(2)]
    attend_items([late_item(chips[:3]), late_item(chips[3:]), early], piece, own_ref)


def attend_cost(queries, keys):
    return pl.CostEstimate(
        flops=4 * queries * keys * HEAD_DIM,
        bytes_accessed=2 << 20,
        transcendentals=queries * keys,
    )


def attend_early(lengths, links, own, keep, come):
    smem, vmem = pl.BlockSpec(memory_space=pltpu.SMEM), pl.BlockSpec(memory_space=pltpu.VMEM)
    return pl.pallas_call(
        attend_early_kernel,
        in_specs=[smem, smem] + [vmem] * 3,
        out_specs=[vmem] * 2,
        out_shape=[
            jax.ShapeDtypeStruct((EARLY, 2 * HEAD_DIM), jnp.float32),
            jax.ShapeDtypeStruct((EARLY, HEAD_DIM), jnp.float32),
        ],
        compiler_params=pltpu.CompilerParams(vmem_limit_bytes=12 << 20),
        cost_estimate=attend_cost(EARLY, LMAX),
        name="attend_early",
    )(lengths, links, own, keep, come)


def attend_late(lengths, links, own, rest, keep, come, sums, tops, far):
    smem, vmem = pl.BlockSpec(memory_space=pltpu.SMEM), pl.BlockSpec(memory_space=pltpu.VMEM)
    shape = (own.shape[0], own.shape[1] // 2, HEAD_DIM)
    return pl.pallas_call(
        attend_late_kernel,
        in_specs=[smem, smem] + [vmem] * (6 + ROUNDS),
        out_specs=vmem,
        out_shape=jax.ShapeDtypeStruct(shape, jnp.bfloat16),
        compiler_params=pltpu.CompilerParams(vmem_limit_bytes=VMEM_BYTES),
        cost_estimate=attend_cost(LMAX - EARLY, LMAX + ROUNDS * FAR),
        name="attend_late",
    )(lengths, links, own, rest, keep, come, sums, tops, *far)


def swap(array):
    return lax.all_to_all(array, "head", split_axis=0, concat_axis=0, tiled=True)


def from_partner(array, bit):
    count = lax.axis_size("shot")
    return lax.ppermute(array, "shot", [(low, low ^ bit) for low in range(count)])


def body(queries, key_rows, value_rows, shot_lengths, shot_links, block_select):
    own = swap(split_heads(key_rows[0], value_rows[0], vmem_bytes=LARGE_BYTES))
    keep, come, rest = gather_queries(queries[0])
    far = [
        from_partner(picked, SHOTS >> (round_index + 1))
        for round_index, picked in enumerate(pick_blocks(block_select, own))
    ]
    sums, tops = attend_early(shot_lengths, shot_links, own, keep, come)
    result = attend_late(shot_lengths, shot_links, own, rest, keep, come, sums, tops, far)
    return join_heads(swap(result))[None]


def solution(mesh):
    placed = (
        P("shot", "head", None),
        P("shot", "head", None),
        P("shot", "head", None),
        P(),
        P(),
        P(),
    )
    return jax.shard_map(
        body, mesh=mesh, in_specs=placed, out_specs=P("shot", "head", None), check_vma=False
    )
```
